32 devices in a mesh: blk: 8 (over z, y), rep: 4 (over x, core).
Axes of the slice: x: 2, y: 2, z: 4, core: 2. Of those that a mesh axis runs over, the one named last changes fastest.
Arguments:
- tensor_blocks: bfloat16 [64, 128, 128, 128], P(('blk', 'rep')), may hold values from -15 to 15
- triples: int32 [64, 3], P(('blk', 'rep')), may hold values from 0 to 15, as said below
- slot_count: int32 [32], P(('blk', 'rep')), may hold values from 1 to 2, as said below
- factor: bfloat16 [2048, 256], P('blk', 'rep'), may hold values from -0.34375 to 0.34375
Outputs:
- gradient: float32 [2048, 256], P('blk', 'rep')
The draws below stay inside these ranges and needn't reach their ends.
Inputs may be any that keep to these rules, and one draw needn't show every extreme that they name: `triples`: each row is i >= j >= k; equal indices occur; the different row blocks named by the 2 slots of one device have different values of block // 2. `slot_count`: the first device's entry is 2.
All inputs are finite; a program needn't handle non-finite values.
Results may differ from the reference program's by a relative error of at most 0.003.
Values may be sent and summed in bfloat16 or wider, within the bound.
A program may use at most 128 MiB of HBM per device.

```python
import jax
import jax.numpy as jnp
from jax import lax

BS = 128
R = 256
BLK_DEV = 2
SLOTS = 2
NB = 16
MODES = 2048
HOLDERS = 32


def draw_triples(key, part):
    keys = jax.random.split(jax.random.fold_in(key, 11), 5)
    owner_total = NB // BLK_DEV
    scores = jax.random.randint(keys[0], (HOLDERS, owner_total), 0, 1 << 20)
    scores = scores * owner_total + jnp.arange(owner_total, dtype=jnp.int32)[None, :]
    owners = jnp.argsort(scores, axis=1)[:, :3 * SLOTS].astype(jnp.int32)
    local = jax.random.randint(keys[1], (HOLDERS, 3 * SLOTS), 0, BLK_DEV)
    picks = (owners * BLK_DEV + local).reshape(HOLDERS * SLOTS, 3)
    first_raw = picks[:, 0]
    second_raw = picks[:, 1]
    third_raw = picks[:, 2]
    shape = (HOLDERS * SLOTS,)
    tie_upper = jax.random.randint(keys[3], shape, 0, 4) == 0
    tie_lower = jax.random.randint(keys[4], shape, 0, 4) == 0
    second_raw = jnp.where(tie_upper, first_raw, second_raw)
    third_raw = jnp.where(tie_lower, second_raw, third_raw)
    highest = jnp.maximum(jnp.maximum(first_raw, second_raw), third_raw)
    lowest = jnp.minimum(jnp.minimum(first_raw, second_raw), third_raw)
    middle = first_raw + second_raw + third_raw - highest - lowest
    return jnp.stack([highest, middle, lowest], axis=1).astype(jnp.int32)


def draw_slot_count(key, part):
    counts = jax.random.randint(jax.random.fold_in(key, 23), (HOLDERS,), 1, SLOTS + 1)
    return counts.at[0].set(SLOTS).astype(jnp.int32)


def draw_factor(key, part):
    keys = jax.random.split(jax.random.fold_in(key, 37), 3)
    scale = (8.0 * MODES * MODES) ** (-0.2)
    noise = jnp.clip(jax.random.normal(keys[0], (MODES, R), jnp.float32), -6.0, 6.0)
    shared = jnp.clip(jax.random.normal(keys[1], (MODES, 1), jnp.float32), -6.0, 6.0)
    column_scale = jax.random.uniform(keys[2], (1, R), jnp.float32, 0.5, 1.5)
    values = noise + 0.5 * shared * column_scale
    return (scale * values).astype(jnp.bfloat16)


def block_scale(rng, dims, pieces, least, top_value):
    gain, own = 1.0, jax.random.fold_in(rng, 6)
    for axis_at, shards_of in pieces:
        steps = jnp.exp(jax.random.uniform(jax.random.fold_in(own, axis_at), (shards_of,), jnp.float32, least / len(pieces), top_value / len(pieces)))
        gain = gain * jnp.repeat(steps, dims[axis_at] // shards_of).reshape([-1 if axis == axis_at else 1 for axis in range(len(dims))])
    return gain


def centred(rng, shape, scale, reach, cuts=(), held_as=jnp.bfloat16):
    factor_of = block_scale(rng, shape, cuts, -0.22, 0.18) if cuts else 1.0
    values = jax.random.normal(rng, shape, jnp.float32) * scale * factor_of
    return jnp.minimum(jnp.maximum(values, -reach), reach).astype(held_as)


def setup_inputs(seed: int = 0) -> dict:
    splits = jax.random.split(jax.random.key(seed), 5)
    tensor_blocks = centred(splits[0], (HOLDERS * SLOTS, BS, BS, BS), 3.0, 15.0, ((0, 32),))
    triples = draw_triples(jax.random.fold_in(splits[4], 71), 0)
    slot_count = draw_slot_count(jax.random.fold_in(splits[4], 71), 0)
    factor = draw_factor(jax.random.fold_in(splits[4], 71), 0)
    return {"tensor_blocks": tensor_blocks, "triples": triples, "slot_count": slot_count, "factor": factor}


def side_weights(triples):
    first_idx = triples[:, 0]
    second_idx = triples[:, 1]
    third_idx = triples[:, 2]
    same_upper = first_idx == second_idx
    same_lower = second_idx == third_idx
    apart = jnp.logical_and(jnp.logical_not(same_upper), jnp.logical_not(same_lower))
    every = jnp.logical_and(same_upper, same_lower)
    base = jnp.where(apart, 2.0, 1.0).astype(jnp.float32)
    dropped = jnp.where(every, 0.0, base).astype(jnp.float32)
    return jnp.stack([base, dropped, dropped], axis=1)


def contract(block, upper, middle, lower):
    edge_size = block.shape[0]
    rank_width = upper.shape[1]
    by_lower = jnp.dot(block.reshape(edge_size * edge_size, edge_size), lower,
                       preferred_element_type=jnp.float32,
                       precision=lax.Precision.HIGHEST).reshape(edge_size, edge_size, rank_width)
    by_upper = lax.dot_general(block.reshape(edge_size, edge_size * edge_size), upper,
                               (((0,), (0,)), ((), ())), preferred_element_type=jnp.float32,
                               precision=lax.Precision.HIGHEST).reshape(edge_size, edge_size, rank_width)
    upper_wide = upper.astype(jnp.float32)
    middle_wide = middle.astype(jnp.float32)
    to_first = jnp.einsum("abr,br->ar", by_lower, middle_wide, precision=lax.Precision.HIGHEST)
    to_second = jnp.einsum("abr,ar->br", by_lower, upper_wide, precision=lax.Precision.HIGHEST)
    to_third = jnp.einsum("bcr,br->cr", by_upper, middle_wide, precision=lax.Precision.HIGHEST)
    return to_first, to_second, to_third


def reference(tensor_blocks, triples, slot_count, factor):
    blocks = factor.astype(jnp.float32).reshape(NB, BS, R)
    slot_ids = jnp.arange(HOLDERS * SLOTS, dtype=jnp.int32)
    holder_of = (slot_ids // SLOTS).astype(jnp.int32)
    position = (slot_ids % SLOTS).astype(jnp.int32)
    alive = (position < slot_count[holder_of]).astype(jnp.float32)
    weights = side_weights(triples) * alive[:, None]

    def accumulate(total, block, triple, weight):
        upper = blocks[triple[0]]
        middle = blocks[triple[1]]
        lower = blocks[triple[2]]
        to_first, to_second, to_third = contract(block.astype(jnp.float32), upper, middle, lower)
        total = total.at[triple[0]].add(weight[0] * to_first)
        total = total.at[triple[1]].add(weight[1] * to_second)
        total = total.at[triple[2]].add(weight[2] * to_third)
        return total

    def step(total, item):
        block, triple, weight, flag = item
        total = lax.cond(flag > 0.5,
                         lambda accum: accumulate(accum, block, triple, weight),
                         lambda accum: accum, total)
        return total, None

    start = jnp.zeros((NB, BS, R), jnp.float32)
    moment, _ = lax.scan(step, start, (tensor_blocks, triples, weights, alive))
    gram = jnp.dot(factor.T, factor, preferred_element_type=jnp.float32)
    hadamard = gram * gram
    fitted = jnp.dot(factor.astype(jnp.float32), hadamard, preferred_element_type=jnp.float32,
                     precision=lax.Precision.HIGHEST)
    return fitted - moment.reshape(MODES, R)
```

```python
import functools

import jax
import jax.numpy as jnp
from jax import lax
from jax.experimental import pallas as pl
from jax.experimental.pallas import tpu as pltpu
from jax.sharding import PartitionSpec as P


def side_weights(triples):
    first_idx = triples[:, 0]
    second_idx = triples[:, 1]
    third_idx = triples[:, 2]
    same_upper = first_idx == second_idx
    same_lower = second_idx == third_idx
    apart = jnp.logical_and(jnp.logical_not(same_upper), jnp.logical_not(same_lower))
    every = jnp.logical_and(same_upper, same_lower)
    base = jnp.where(apart, 2.0, 1.0).astype(jnp.float32)
    dropped = jnp.where(every, 0.0, base)
    return jnp.stack([base, dropped, dropped], axis=1)


def contract_kernel(chunk, group, per_owner, trip_ref, w_ref, tab_ref, x_ref, out_ref, fi, fj, y1, y2, y3):
    s = pl.program_id(0)
    step = pl.program_id(1)
    i = trip_ref[s, 0]
    j = trip_ref[s, 1]
    k = trip_ref[s, 2]

    @pl.when(jnp.logical_and(s == 0, step == 0))
    def _():
        out_ref[...] = jnp.zeros_like(out_ref)

    @pl.when(step == 0)
    def _():
        fi[...] = tab_ref[i].astype(jnp.float32)
        fj[...] = tab_ref[j].astype(jnp.float32)
        y2[...] = jnp.zeros_like(y2)
        y3[...] = jnp.zeros_like(y3)

    middle = tab_ref[j]
    lower = tab_ref[k]

    @pl.loop(0, chunk // group)
    def _(g):
        start = pl.multiple_of(step * chunk + g * group, group)
        scale = fi[pl.ds(start, group), :]
        rows = []
        second = y2[...]
        third = y3[...]
        for u in range(group):
            block = x_ref[0, g * group + u]
            left = jnp.dot(block, lower, preferred_element_type=jnp.float32)
            right = lax.dot_general(
                block, middle, (((0,), (0,)), ((), ())), preferred_element_type=jnp.float32
            )
            line = scale[u : u + 1, :]
            second = second + left * line
            third = third + right * line
            rows.append(jnp.sum(left * fj[...], axis=0, keepdims=True))
        y2[...] = second
        y3[...] = third
        y1[pl.ds(start, group), :] = jnp.concatenate(rows, axis=0)

    @pl.when(step == pl.num_programs(1) - 1)
    def _():
        out_ref[i // per_owner] += w_ref[s, 0] * y1[...]
        out_ref[j // per_owner] += w_ref[s, 1] * y2[...]
        out_ref[k // per_owner] += w_ref[s, 2] * y3[...]


def contract_all(triples, weights, table, tensor_blocks, owner_count, per_owner):
    slots, edge = tensor_blocks.shape[:2]
    rank = table.shape[2]
    chunk = 32
    group = 8
    wide = pltpu.VMEM((edge, rank), jnp.float32)
    return pl.pallas_call(
        functools.partial(contract_kernel, chunk, group, per_owner),
        grid=(slots, edge // chunk),
        out_shape=jax.ShapeDtypeStruct((owner_count, edge, rank), jnp.float32),
        in_specs=[
            pl.BlockSpec(memory_space=pltpu.SMEM),
            pl.BlockSpec(memory_space=pltpu.SMEM),
            pl.BlockSpec(memory_space=pltpu.VMEM),
            pl.BlockSpec((1, chunk, edge, edge), lambda s, t: (s, t, 0, 0)),
        ],
        out_specs=pl.BlockSpec(memory_space=pltpu.VMEM),
        scratch_shapes=[wide] * 5,
        compiler_params=pltpu.CompilerParams(vmem_limit_bytes=40 * 1024 * 1024),
    )(triples, weights, table, tensor_blocks)


def owned_table(listed, owner_count, per_owner):
    myself = lax.axis_index("blk")
    flat = listed.reshape(owner_count, -1)
    mine = flat // per_owner == myself
    local = flat % per_owner
    column_ids = jnp.arange(per_owner, dtype=jnp.int32)
    hits = jnp.logical_and(mine[:, :, None], local[:, :, None] == column_ids[None, None, :])
    return jnp.any(hits, axis=1)


def shards(tensor_blocks, triples, slot_count, factor):
    own_rows = lax.all_gather(factor, "rep", axis=1, tiled=True)
    listed_back = lax.all_gather(triples, "blk", axis=0, tiled=True)
    block_size = tensor_blocks.shape[1]
    rank_width = own_rows.shape[1]
    owner_count = lax.axis_size("blk")
    per_owner = own_rows.shape[0] // block_size
    block_count = owner_count * per_owner
    gathered = lax.all_gather(own_rows, "blk", axis=0, tiled=True)
    gathered, listed_back = lax.optimization_barrier((gathered, listed_back))
    table = gathered.reshape(block_count, block_size, rank_width)
    slot_total = tensor_blocks.shape[0]
    alive = (jnp.arange(slot_total, dtype=jnp.int32) < slot_count[0]).astype(jnp.float32)
    weights = side_weights(triples) * alive[:, None]
    outgoing_sums = contract_all(triples, weights, table, tensor_blocks, owner_count, per_owner)
    arrived = lax.all_to_all(outgoing_sums, "blk", split_axis=0, concat_axis=0, tiled=True)
    gram_matrix = lax.dot_general(
        gathered, gathered, (((0,), (0,)), ((), ())), preferred_element_type=jnp.float32
    )
    hadamard = gram_matrix * gram_matrix
    column_width = factor.shape[1]
    column_start = lax.axis_index("rep") * column_width
    hadamard_cols = lax.dynamic_slice_in_dim(hadamard, column_start, column_width, 1)
    fitted = jnp.dot(
        own_rows.astype(jnp.float32),
        hadamard_cols,
        preferred_element_type=jnp.float32,
        precision=lax.Precision.HIGHEST,
    )
    placing = owned_table(listed_back, owner_count, per_owner).astype(jnp.float32)
    owned = jnp.einsum("ql,qar->lar", placing, arrived, precision=lax.Precision.HIGHEST).reshape(
        per_owner * block_size, rank_width
    )
    owned_sum = lax.psum_scatter(owned, "rep", scatter_dimension=1, tiled=True)
    return fitted - owned_sum


def solution(mesh):
    in_specs = (
        P(("blk", "rep"), None, None, None),
        P(("blk", "rep"), None),
        P(("blk", "rep")),
        P("blk", "rep"),
    )
    out_specs = P("blk", "rep")
    return jax.shard_map(shards, mesh=mesh, in_specs=in_specs, out_specs=out_specs, check_vma=False)
```

```python
import functools

import jax
import jax.numpy as jnp
from jax import lax
from jax.experimental import pallas as pl
from jax.experimental.pallas import tpu as pltpu
from jax.sharding import PartitionSpec as P


def side_weights(triples):
    first_idx = triples[:, 0]
    second_idx = triples[:, 1]
    third_idx = triples[:, 2]
    same_upper = first_idx == second_idx
    same_lower = second_idx == third_idx
    apart = jnp.logical_and(jnp.logical_not(same_upper), jnp.logical_not(same_lower))
    every = jnp.logical_and(same_upper, same_lower)
    base = jnp.where(apart, 2.0, 1.0).astype(jnp.float32)
    dropped = jnp.where(every, 0.0, base)
    return jnp.stack([base, dropped, dropped], axis=1)


MESH = pl.DeviceIdType.MESH


def bits_of(size):
    return [1 << p for p in range(size.bit_length() - 1)]


def flip(index, bit):
    return index + bit - 2 * bit * ((index // bit) % 2)


def place(rep, blk, combo):
    for (axis, bit), on in combo:
        if on:
            if axis == "rep":
                rep = flip(rep, bit)
            else:
                blk = flip(blk, bit)
    return rep, blk


def combos(steps):
    found = [()]
    for step in steps:
        found = [c + ((step, on),) for c in found for on in (1, 0)]
    return found


def greet(steps, rep, blk):
    barrier = pltpu.get_barrier_semaphore()
    for step in steps:
        to_rep, to_blk = place(rep, blk, ((step, 1),))
        pl.semaphore_signal(barrier, inc=1, device_id=(to_blk, to_rep), device_id_type=MESH)
    pl.semaphore_wait(barrier, len(steps))


def gather_kernel(steps, own_ref, all_ref, send_sem, recv_sem):
    rep = lax.axis_index("rep")
    blk = lax.axis_index("blk")
    greet(steps, rep, blk)
    all_ref[rep, blk] = own_ref[...]
    sent = []

    def copy(at, combo, index):
        src_rep, src_blk = place(rep, blk, combo)
        to_rep, to_blk = place(rep, blk, ((steps[at], 1),))
        where = all_ref.at[src_rep, src_blk]
        return pltpu.make_async_remote_copy(
            src_ref=where,
            dst_ref=where,
            send_sem=send_sem.at[at, index],
            recv_sem=recv_sem.at[at, index],
            device_id=(to_blk, to_rep),
            device_id_type=MESH,
        )

    def spread(first, combo):
        for at in range(first, len(steps)):
            full = combo + tuple((s, 0) for s in steps[len(combo):at])
            out = copy(at, full, combos(steps[:at])[::-1].index(full))
            out.start()
            sent.append(out)

    spread(0, ())
    for at in range(len(steps)):
        for index, combo in enumerate(combos(steps[:at])[::-1]):
            mine = combo + ((steps[at], 1),)
            copy(at, mine, index).wait_recv()
            spread(at + 1, mine)
    for out in sent:
        out.wait_send()


def reduce_kernel(steps, part_ref, out_ref, acc, land, send_sem, recv_sem):
    rep = lax.axis_index("rep")
    blk = lax.axis_index("blk")
    greet(steps, rep, blk)
    base = [0]
    for at in range(len(steps)):
        base.append(base[-1] + (1 << (len(steps) - 1 - at)))

    def copy(at, combo, index):
        src_rep, src_blk = place(rep, blk, ((steps[at], 1),) + combo)
        to_rep, to_blk = place(rep, blk, ((steps[at], 1),))
        slot = base[at] + index
        source = part_ref if at == 0 else acc
        return pltpu.make_async_remote_copy(
            src_ref=source.at[src_rep, src_blk],
            dst_ref=land.at[slot],
            send_sem=send_sem.at[slot],
            recv_sem=recv_sem.at[slot],
            device_id=(to_blk, to_rep),
            device_id_type=MESH,
        )

    sent = []
    for index, combo in enumerate(combos(steps[1:])):
        out = copy(0, combo, index)
        out.start()
        sent.append(out)
    for at in range(len(steps)):
        later = combos(steps[at + 2:])
        for index, combo in enumerate(combos(steps[at + 1:])):
            copy(at, combo, index).wait_recv()
            at_rep, at_blk = place(rep, blk, combo)
            held = part_ref if at == 0 else acc
            total = held[at_rep, at_blk] + land[base[at] + index]
            if at == len(steps) - 1:
                out_ref[...] = total
            else:
                acc[at_rep, at_blk] = total
                if combo[0][1]:
                    out = copy(at + 1, combo[1:], later.index(combo[1:]))
                    out.start()
                    sent.append(out)
    for out in sent:
        out.wait_send()


def gather_all(own, rep_count, blk_count):
    steps = [("blk", b) for b in bits_of(blk_count)[::-1]] + [("rep", b) for b in bits_of(rep_count)[::-1]]
    most = max(1, rep_count * blk_count // 2)
    return pl.pallas_call(
        functools.partial(gather_kernel, steps),
        out_shape=jax.ShapeDtypeStruct((rep_count, blk_count) + own.shape, own.dtype),
        in_specs=[pl.BlockSpec(memory_space=pltpu.VMEM)],
        out_specs=pl.BlockSpec(memory_space=pltpu.VMEM),
        scratch_shapes=[
            pltpu.SemaphoreType.DMA((len(steps), most)),
            pltpu.SemaphoreType.DMA((len(steps), most)),
        ],
        compiler_params=pltpu.CompilerParams(
            collective_id=0, has_side_effects=True, vmem_limit_bytes=40 * 1024 * 1024
        ),
    )(own)


def reduce_all(parts):
    rep_count, blk_count = parts.shape[:2]
    steps = [("rep", b) for b in bits_of(rep_count)] + [("blk", b) for b in bits_of(blk_count)]
    total = rep_count * blk_count - 1
    piece = parts.shape[2:]
    return pl.pallas_call(
        functools.partial(reduce_kernel, steps),
        out_shape=jax.ShapeDtypeStruct(piece, parts.dtype),
        in_specs=[pl.BlockSpec(memory_space=pltpu.VMEM)],
        out_specs=pl.BlockSpec(memory_space=pltpu.VMEM),
        scratch_shapes=[
            pltpu.VMEM(parts.shape, parts.dtype),
            pltpu.VMEM((total,) + piece, parts.dtype),
            pltpu.SemaphoreType.DMA((total,)),
            pltpu.SemaphoreType.DMA((total,)),
        ],
        compiler_params=pltpu.CompilerParams(
            collective_id=1, has_side_effects=True, vmem_limit_bytes=48 * 1024 * 1024
        ),
    )(parts)


def contract_kernel(
    chunk, group, per_owner, cols, trip_ref, w_ref, tab_ref, x_ref, out_ref, fi, fj, fk, y1, y2, y3
):
    s = pl.program_id(0)
    step = pl.program_id(1)
    depth, lanes = tab_ref.shape[2:]
    edge, rank = fi.shape
    fold = lanes // cols
    groups = edge // depth
    lane_group = lax.broadcasted_iota(jnp.int32, (depth, lanes), 1) // cols

    def load_block(index, dest):
        owner = index // per_owner
        for u in range(groups):
            g = (index % per_owner) * groups + u
            for h in range(rank // lanes):
                tile = jnp.zeros((depth, lanes), jnp.float32)
                for m in range(fold):
                    piece = tab_ref[h * fold + m, owner].astype(jnp.float32)
                    moved = pltpu.roll(piece, ((m + fold - g) % fold) * cols, 1)
                    tile = jnp.where(lane_group == m, moved, tile)
                dest[u * depth : (u + 1) * depth, h * lanes : (h + 1) * lanes] = tile.astype(dest.dtype)

    def add_block(index, weight, value):
        owner = index // per_owner
        for u in range(groups):
            g = (index % per_owner) * groups + u
            for h in range(rank // lanes):
                tile = weight * value[u * depth : (u + 1) * depth, h * lanes : (h + 1) * lanes]
                for m in range(fold):
                    moved = pltpu.roll(tile, ((g + fold - m) % fold) * cols, 1)
                    out_ref[h * fold + m, owner] += jnp.where(lane_group == g, moved, 0.0)

    i = trip_ref[s, 0]
    j = trip_ref[s, 1]
    k = trip_ref[s, 2]

    @pl.when(jnp.logical_and(s == 0, step == 0))
    def _():
        out_ref[...] = jnp.zeros_like(out_ref)

    @pl.when(step == 0)
    def _():
        load_block(i, fi)
        load_block(j, fj)
        load_block(k, fk)
        y2[...] = jnp.zeros_like(y2)
        y3[...] = jnp.zeros_like(y3)

    middle = fj[...].astype(jnp.bfloat16)
    lower = fk[...].astype(jnp.bfloat16)

    @pl.loop(0, chunk // group)
    def _(g):
        start = pl.multiple_of(step * chunk + g * group, group)
        scale = fi[pl.ds(start, group), :]
        rows = []
        second = y2[...]
        third = y3[...]
        for u in range(group):
            block = x_ref[0, g * group + u]
            left = jnp.dot(block, lower, preferred_element_type=jnp.float32)
            right = lax.dot_general(
                block, middle, (((0,), (0,)), ((), ())), preferred_element_type=jnp.float32
            )
            line = scale[u : u + 1, :]
            second = second + left * line
            third = third + right * line
            rows.append(jnp.sum(left * fj[...], axis=0, keepdims=True))
        y2[...] = second
        y3[...] = third
        y1[pl.ds(start, group), :] = jnp.concatenate(rows, axis=0)

    @pl.when(step == pl.num_programs(1) - 1)
    def _():
        add_block(i, w_ref[s, 0], y1)
        add_block(j, w_ref[s, 1], y2)
        add_block(k, w_ref[s, 2], y3)


def contract_all(triples, weights, table, tensor_blocks, per_owner, cols, rank):
    slots, edge = tensor_blocks.shape[:2]
    chunk = 32
    group = 8
    wide = pltpu.VMEM((edge, rank), jnp.float32)
    return pl.pallas_call(
        functools.partial(contract_kernel, chunk, group, per_owner, cols),
        grid=(slots, edge // chunk),
        out_shape=jax.ShapeDtypeStruct(table.shape, jnp.float32),
        in_specs=[
            pl.BlockSpec(memory_space=pltpu.SMEM),
            pl.BlockSpec(memory_space=pltpu.SMEM),
            pl.BlockSpec(memory_space=pltpu.VMEM),
            pl.BlockSpec((1, chunk, edge, edge), lambda s, t: (s, t, 0, 0)),
        ],
        out_specs=pl.BlockSpec(memory_space=pltpu.VMEM),
        scratch_shapes=[wide] * 6,
        compiler_params=pltpu.CompilerParams(vmem_limit_bytes=48 * 1024 * 1024),
    )(triples, weights, table, tensor_blocks)


def shards(tensor_blocks, triples, slot_count, factor):
    rows, cols = factor.shape
    edge = tensor_blocks.shape[1]
    rep_count = lax.axis_size("rep")
    blk_count = lax.axis_size("blk")
    rank = cols * rep_count
    fold = 128 // cols
    depth = rows // fold
    packed = factor.reshape(fold, depth, cols).transpose(1, 0, 2).reshape(depth, fold * cols)
    table = gather_all(packed, rep_count, blk_count)
    slot_total = tensor_blocks.shape[0]
    alive = (jnp.arange(slot_total, dtype=jnp.int32) < slot_count[0]).astype(jnp.float32)
    weights = side_weights(triples) * alive[:, None]
    parts = contract_all(triples, weights, table, tensor_blocks, rows // edge, cols, rank)
    moment = reduce_all(parts)
    moment = moment.reshape(depth, fold, cols).transpose(1, 0, 2).reshape(rows, cols)

    flat = table.reshape(rep_count, blk_count * depth, fold * cols)
    mine = lax.dynamic_index_in_dim(flat, lax.axis_index("rep"), 0, keepdims=False)
    pairs = lax.dot_general(
        flat, mine, (((1,), (0,)), ((), ())), preferred_element_type=jnp.float32
    )
    gram_cols = sum(
        pairs[:, g * cols : (g + 1) * cols, g * cols : (g + 1) * cols] for g in range(fold)
    ).reshape(rank, cols)
    own = lax.dynamic_index_in_dim(table, lax.axis_index("blk"), 1, keepdims=False)
    own_rows = own.reshape(rep_count, depth, fold, cols).transpose(2, 1, 0, 3).reshape(rows, rank)
    fitted = jnp.dot(
        own_rows.astype(jnp.float32),
        gram_cols * gram_cols,
        preferred_element_type=jnp.float32,
        precision=lax.Precision.HIGHEST,
    )
    return fitted - moment


def solution(mesh):
    in_specs = (
        P(("blk", "rep"), None, None, None),
        P(("blk", "rep"), None),
        P(("blk", "rep")),
        P("blk", "rep"),
    )
    out_specs = P("blk", "rep")
    return jax.shard_map(shards, mesh=mesh, in_specs=in_specs, out_specs=out_specs, check_vma=False)
```

```python
import functools

import jax
import jax.numpy as jnp
from jax import lax
from jax.experimental import pallas as pl
from jax.experimental.pallas import tpu as pltpu
from jax.sharding import PartitionSpec as P


MESH = pl.DeviceIdType.MESH


def bits_of(size):
    return [1 << p for p in range(size.bit_length() - 1)]


def flip(index, bit):
    return index + bit - 2 * bit * ((index // bit) % 2)


def place(rep, blk, combo):
    for (axis, bit), on in combo:
        if on:
            if axis == "rep":
                rep = flip(rep, bit)
            else:
                blk = flip(blk, bit)
    return rep, blk


def combos(steps):
    found = [()]
    for step in steps:
        found = [c + ((step, on),) for c in found for on in (1, 0)]
    return found


def greet(steps, rep, blk):
    barrier = pltpu.get_barrier_semaphore()
    for step in steps:
        to_rep, to_blk = place(rep, blk, ((step, 1),))
        pl.semaphore_signal(barrier, inc=1, device_id=(to_blk, to_rep), device_id_type=MESH)
    pl.semaphore_wait(barrier, len(steps))


def gather_kernel(orders, own_ref, all_ref, send_sem, recv_sem):
    rep = lax.axis_index("rep")
    blk = lax.axis_index("blk")
    greet(orders[0], rep, blk)
    all_ref[rep, blk] = own_ref[...]
    share = own_ref.shape[0] // len(orders)
    sent = []

    def copy(part, at, combo, index):
        steps = orders[part]
        src_rep, src_blk = place(rep, blk, combo)
        to_rep, to_blk = place(rep, blk, ((steps[at], 1),))
        where = all_ref.at[src_rep, src_blk, pl.ds(part * share, share)]
        return pltpu.make_async_remote_copy(
            src_ref=where,
            dst_ref=where,
            send_sem=send_sem.at[part, (1 << at) - 1 + index],
            recv_sem=recv_sem.at[part, (1 << at) - 1 + index],
            device_id=(to_blk, to_rep),
            device_id_type=MESH,
        )

    def spread(part, first, combo):
        steps = orders[part]
        for at in range(first, len(steps)):
            full = combo + tuple((s, 0) for s in steps[len(combo):at])
            out = copy(part, at, full, combos(steps[:at])[::-1].index(full))
            out.start()
            sent.append(out)

    for part in range(len(orders)):
        spread(part, 0, ())
    for at in range(len(orders[0])):
        for index in range(1 << at):
            for part, steps in enumerate(orders):
                mine = combos(steps[:at])[::-1][index] + ((steps[at], 1),)
                copy(part, at, mine, index).wait_recv()
                spread(part, at + 1, mine)
    for out in sent:
        out.wait_send()


def reduce_kernel(orders, part_ref, out_ref, acc, land, send_sem, recv_sem):
    rep = lax.axis_index("rep")
    blk = lax.axis_index("blk")
    greet(orders[0], rep, blk)
    share = out_ref.shape[0] // len(orders)
    count = len(orders[0])
    base = [0]
    for at in range(count):
        base.append(base[-1] + (1 << (count - 1 - at)))

    def copy(part, at, combo, index):
        step = orders[part][at]
        src_rep, src_blk = place(rep, blk, ((step, 1),) + combo)
        to_rep, to_blk = place(rep, blk, ((step, 1),))
        slot = base[at] + index
        source = part_ref if at == 0 else acc
        rows = pl.ds(part * share, share)
        return pltpu.make_async_remote_copy(
            src_ref=source.at[src_rep, src_blk, rows],
            dst_ref=land.at[slot, rows],
            send_sem=send_sem.at[part, slot],
            recv_sem=recv_sem.at[part, slot],
            device_id=(to_blk, to_rep),
            device_id_type=MESH,
        )

    sent = []
    for index in range(1 << (count - 1)):
        for part, steps in enumerate(orders):
            out = copy(part, 0, combos(steps[1:])[index], index)
            out.start()
            sent.append(out)
    for at in range(count):
        for index in range(1 << (count - 1 - at)):
            for part, steps in enumerate(orders):
                combo = combos(steps[at + 1:])[index]
                copy(part, at, combo, index).wait_recv()
                at_rep, at_blk = place(rep, blk, combo)
                held = part_ref if at == 0 else acc
                rows = pl.ds(part * share, share)
                total = held[at_rep, at_blk, rows] + land[base[at] + index, rows]
                if at == count - 1:
                    out_ref[rows] = total
                else:
                    acc[at_rep, at_blk, rows] = total
                    if combo[0][1]:
                        later = combos(steps[at + 2:])
                        out = copy(part, at + 1, combo[1:], later.index(combo[1:]))
                        out.start()
                        sent.append(out)
    for out in sent:
        out.wait_send()


def gather_all(own, rep_count, blk_count):
    blks = [("blk", b) for b in bits_of(blk_count)[::-1]]
    reps = [("rep", b) for b in bits_of(rep_count)[::-1]]
    orders = [blks + reps, blks[:-1] + reps[:-1] + blks[-1:] + reps[-1:]]
    total = rep_count * blk_count - 1
    return pl.pallas_call(
        functools.partial(gather_kernel, orders),
        out_shape=jax.ShapeDtypeStruct((rep_count, blk_count) + own.shape, own.dtype),
        in_specs=[pl.BlockSpec(memory_space=pltpu.VMEM)],
        out_specs=pl.BlockSpec(memory_space=pltpu.VMEM),
        scratch_shapes=[
            pltpu.SemaphoreType.DMA((len(orders), total)),
            pltpu.SemaphoreType.DMA((len(orders), total)),
        ],
        compiler_params=pltpu.CompilerParams(
            collective_id=0, has_side_effects=True, vmem_limit_bytes=40 * 1024 * 1024
        ),
    )(own)


def reduce_all(parts):
    rep_count, blk_count = parts.shape[:2]
    blks = [("blk", b) for b in bits_of(blk_count)]
    reps = [("rep", b) for b in bits_of(rep_count)]
    orders = [reps + blks, reps[:1] + blks[:1] + reps[1:] + blks[1:]]
    total = rep_count * blk_count - 1
    piece = parts.shape[2:]
    return pl.pallas_call(
        functools.partial(reduce_kernel, orders),
        out_shape=jax.ShapeDtypeStruct(piece, parts.dtype),
        in_specs=[pl.BlockSpec(memory_space=pltpu.VMEM)],
        out_specs=pl.BlockSpec(memory_space=pltpu.VMEM),
        scratch_shapes=[
            pltpu.VMEM(parts.shape, parts.dtype),
            pltpu.VMEM((total,) + piece, parts.dtype),
            pltpu.SemaphoreType.DMA((len(orders), total)),
            pltpu.SemaphoreType.DMA((len(orders), total)),
        ],
        compiler_params=pltpu.CompilerParams(
            collective_id=1, has_side_effects=True, vmem_limit_bytes=48 * 1024 * 1024
        ),
    )(parts)


def contract_kernel(
    chunk, group, per_owner, cols, trip_ref, count_ref, tab_ref, x_ref, out_ref, fi, fj, fk, y1, y2, y3
):
    s = pl.program_id(0)
    step = pl.program_id(1)
    depth, lanes = tab_ref.shape[2:]
    edge, rank = fi.shape
    fold = lanes // cols
    groups = edge // depth
    lane_group = lax.broadcasted_iota(jnp.int32, (depth, lanes), 1) // cols

    def load_block(index, dest):
        owner = index // per_owner
        for u in range(groups):
            g = (index % per_owner) * groups + u
            for h in range(rank // lanes):
                tile = jnp.zeros((depth, lanes), jnp.float32)
                for m in range(fold):
                    piece = tab_ref[h * fold + m, owner].astype(jnp.float32)
                    moved = pltpu.roll(piece, ((m + fold - g) % fold) * cols, 1)
                    tile = jnp.where(lane_group == m, moved, tile)
                dest[u * depth : (u + 1) * depth, h * lanes : (h + 1) * lanes] = tile.astype(dest.dtype)

    def add_block(index, weight, value):
        owner = index // per_owner
        for u in range(groups):
            g = (index % per_owner) * groups + u
            for h in range(rank // lanes):
                tile = weight * value[u * depth : (u + 1) * depth, h * lanes : (h + 1) * lanes]
                for m in range(fold):
                    moved = pltpu.roll(tile, ((g + fold - m) % fold) * cols, 1)
                    out_ref[h * fold + m, owner] += jnp.where(lane_group == g, moved, 0.0)

    i = trip_ref[s, 0]
    j = trip_ref[s, 1]
    k = trip_ref[s, 2]

    @pl.when(jnp.logical_and(s == 0, step == 0))
    def _():
        out_ref[...] = jnp.zeros_like(out_ref)

    @pl.when(step == 0)
    def _():
        load_block(i, fi)
        load_block(j, fj)
        load_block(k, fk)
        y2[...] = jnp.zeros_like(y2)
        y3[...] = jnp.zeros_like(y3)

    middle = fj[...].astype(jnp.bfloat16)
    lower = fk[...].astype(jnp.bfloat16)

    @pl.loop(0, chunk // group)
    def _(g):
        start = pl.multiple_of(step * chunk + g * group, group)
        scale = fi[pl.ds(start, group), :]
        rows = []
        second = y2[...]
        third = y3[...]
        for u in range(group):
            block = x_ref[0, g * group + u]
            left = jnp.dot(block, lower, preferred_element_type=jnp.float32)
            right = lax.dot_general(
                block, middle, (((0,), (0,)), ((), ())), preferred_element_type=jnp.float32
            )
            line = scale[u : u + 1, :]
            second = second + left * line
            third = third + right * line
            rows.append(jnp.sum(left * fj[...], axis=0, keepdims=True))
        y2[...] = second
        y3[...] = third
        y1[pl.ds(start, group), :] = jnp.concatenate(rows, axis=0)

    @pl.when(step == pl.num_programs(1) - 1)
    def _():
        apart = jnp.logical_and(i != j, j != k)
        every = jnp.logical_and(i == j, j == k)
        base = jnp.where(s < count_ref[0], jnp.where(apart, 2.0, 1.0), 0.0)
        dropped = jnp.where(every, 0.0, base)
        add_block(i, base, y1)
        add_block(j, dropped, y2)
        add_block(k, dropped, y3)


def contract_all(triples, slot_count, table, tensor_blocks, per_owner, cols, rank):
    slots, edge = tensor_blocks.shape[:2]
    chunk = 32
    group = 8
    wide = pltpu.VMEM((edge, rank), jnp.float32)
    return pl.pallas_call(
        functools.partial(contract_kernel, chunk, group, per_owner, cols),
        grid=(slots, edge // chunk),
        out_shape=jax.ShapeDtypeStruct(table.shape, jnp.float32),
        in_specs=[
            pl.BlockSpec(memory_space=pltpu.SMEM),
            pl.BlockSpec(memory_space=pltpu.SMEM),
            pl.BlockSpec(memory_space=pltpu.VMEM),
            pl.BlockSpec((1, chunk, edge, edge), lambda s, t: (s, t, 0, 0)),
        ],
        out_specs=pl.BlockSpec(memory_space=pltpu.VMEM),
        scratch_shapes=[wide] * 6,
        compiler_params=pltpu.CompilerParams(vmem_limit_bytes=48 * 1024 * 1024),
    )(triples, slot_count, table, tensor_blocks)


def shards(tensor_blocks, triples, slot_count, factor):
    rows, cols = factor.shape
    edge = tensor_blocks.shape[1]
    rep_count = lax.axis_size("rep")
    blk_count = lax.axis_size("blk")
    rank = cols * rep_count
    fold = 128 // cols
    depth = rows // fold
    packed = factor.reshape(fold, depth, cols).transpose(1, 0, 2).reshape(depth, fold * cols)
    table = gather_all(packed, rep_count, blk_count)
    parts = contract_all(triples, slot_count, table, tensor_blocks, rows // edge, cols, rank)
    moment = reduce_all(parts)
    moment = moment.reshape(depth, fold, cols).transpose(1, 0, 2).reshape(rows, cols)

    flat = table.reshape(rep_count, blk_count * depth, fold * cols)
    mine = lax.dynamic_index_in_dim(flat, lax.axis_index("rep"), 0, keepdims=False)
    pairs = lax.dot_general(
        flat, mine, (((1,), (0,)), ((), ())), preferred_element_type=jnp.float32
    )
    gram_cols = sum(
        pairs[:, g * cols : (g + 1) * cols, g * cols : (g + 1) * cols] for g in range(fold)
    ).reshape(rank, cols)
    own = lax.dynamic_index_in_dim(table, lax.axis_index("blk"), 1, keepdims=False)
    own_rows = own.reshape(rep_count, depth, fold, cols).transpose(2, 1, 0, 3).reshape(rows, rank)
    fitted = jnp.dot(
        own_rows.astype(jnp.float32),
        gram_cols * gram_cols,
        preferred_element_type=jnp.float32,
        precision=lax.Precision.HIGHEST,
    )
    return fitted - moment


def solution(mesh):
    in_specs = (
        P(("blk", "rep"), None, None, None),
        P(("blk", "rep"), None),
        P(("blk", "rep")),
        P("blk", "rep"),
    )
    out_specs = P("blk", "rep")
    return jax.shard_map(shards, mesh=mesh, in_specs=in_specs, out_specs=out_specs, check_vma=False)
```

```python
import functools

import jax
import jax.numpy as jnp
from jax import lax
from jax.experimental import pallas as pl
from jax.experimental.pallas import tpu as pltpu
from jax.sharding import PartitionSpec as P


MESH = pl.DeviceIdType.MESH


def bits_of(size):
    return [1 << p for p in range(size.bit_length() - 1)]


def flip(index, bit):
    return index + bit - 2 * bit * ((index // bit) % 2)


def place(rep, blk, combo):
    for (axis, bit), on in combo:
        if on:
            if axis == "rep":
                rep = flip(rep, bit)
            else:
                blk = flip(blk, bit)
    return rep, blk


def combos(steps):
    found = [()]
    for step in steps:
        found = [c + ((step, on),) for c in found for on in (1, 0)]
    return found


def greet(steps, rep, blk):
    barrier = pltpu.get_barrier_semaphore()
    for step in steps:
        to_rep, to_blk = place(rep, blk, ((step, 1),))
        pl.semaphore_signal(barrier, inc=1, device_id=(to_blk, to_rep), device_id_type=MESH)
    pl.semaphore_wait(barrier, len(steps))


def gather_kernel(orders, own_ref, all_ref, send_sem, recv_sem):
    rep = lax.axis_index("rep")
    blk = lax.axis_index("blk")
    greet(orders[0], rep, blk)
    all_ref[rep, blk] = own_ref[...]
    share = own_ref.shape[0] // len(orders)
    sent = []

    def copy(part, at, combo, index):
        steps = orders[part]
        src_rep, src_blk = place(rep, blk, combo)
        to_rep, to_blk = place(rep, blk, ((steps[at], 1),))
        where = all_ref.at[src_rep, src_blk, pl.ds(part * share, share)]
        return pltpu.make_async_remote_copy(
            src_ref=where,
            dst_ref=where,
            send_sem=send_sem.at[part, (1 << at) - 1 + index],
            recv_sem=recv_sem.at[part, (1 << at) - 1 + index],
            device_id=(to_blk, to_rep),
            device_id_type=MESH,
        )

    def spread(part, first, combo):
        steps = orders[part]
        for at in range(first, len(steps)):
            full = combo + tuple((s, 0) for s in steps[len(combo):at])
            out = copy(part, at, full, combos(steps[:at])[::-1].index(full))
            out.start()
            sent.append(out)

    for part in range(len(orders)):
        spread(part, 0, ())
    for at in range(len(orders[0])):
        for index in range(1 << at):
            for part, steps in enumerate(orders):
                mine = combos(steps[:at])[::-1][index] + ((steps[at], 1),)
                copy(part, at, mine, index).wait_recv()
                spread(part, at + 1, mine)
    for out in sent:
        out.wait_send()


def reduce_kernel(orders, part_ref, out_ref, acc, land, send_sem, recv_sem):
    rep = lax.axis_index("rep")
    blk = lax.axis_index("blk")
    greet(orders[0], rep, blk)
    share = out_ref.shape[0] // len(orders)
    count = len(orders[0])
    base = [0]
    for at in range(count):
        base.append(base[-1] + (1 << (count - 1 - at)))

    def copy(part, at, combo, index):
        step = orders[part][at]
        src_rep, src_blk = place(rep, blk, ((step, 1),) + combo)
        to_rep, to_blk = place(rep, blk, ((step, 1),))
        slot = base[at] + index
        source = part_ref if at == 0 else acc
        rows = pl.ds(part * share, share)
        return pltpu.make_async_remote_copy(
            src_ref=source.at[src_rep, src_blk, rows],
            dst_ref=land.at[slot, rows],
            send_sem=send_sem.at[part, slot],
            recv_sem=recv_sem.at[part, slot],
            device_id=(to_blk, to_rep),
            device_id_type=MESH,
        )

    sent = []
    for index in range(1 << (count - 1)):
        for part, steps in enumerate(orders):
            out = copy(part, 0, combos(steps[1:])[index], index)
            out.start()
            sent.append(out)
    for at in range(count):
        for index in range(1 << (count - 1 - at)):
            for part, steps in enumerate(orders):
                combo = combos(steps[at + 1:])[index]
                copy(part, at, combo, index).wait_recv()
                at_rep, at_blk = place(rep, blk, combo)
                held = part_ref if at == 0 else acc
                rows = pl.ds(part * share, share)
                total = held[at_rep, at_blk, rows] + land[base[at] + index, rows]
                if at == count - 1:
                    out_ref[rows] = total
                else:
                    acc[at_rep, at_blk, rows] = total
                    if combo[0][1]:
                        later = combos(steps[at + 2:])
                        out = copy(part, at + 1, combo[1:], later.index(combo[1:]))
                        out.start()
                        sent.append(out)
    for out in sent:
        out.wait_send()


def gather_all(own, rep_count, blk_count):
    blks = [("blk", b) for b in bits_of(blk_count)[::-1]]
    reps = [("rep", b) for b in bits_of(rep_count)[::-1]]
    orders = [blks + reps, blks[:-1] + reps[:-1] + blks[-1:] + reps[-1:]]
    total = rep_count * blk_count - 1
    return pl.pallas_call(
        functools.partial(gather_kernel, orders),
        out_shape=jax.ShapeDtypeStruct((rep_count, blk_count) + own.shape, own.dtype),
        in_specs=[pl.BlockSpec(memory_space=pltpu.VMEM)],
        out_specs=pl.BlockSpec(memory_space=pltpu.VMEM),
        scratch_shapes=[
            pltpu.SemaphoreType.DMA((len(orders), total)),
            pltpu.SemaphoreType.DMA((len(orders), total)),
        ],
        compiler_params=pltpu.CompilerParams(
            collective_id=0, has_side_effects=True, vmem_limit_bytes=40 * 1024 * 1024
        ),
    )(own)


def reduce_all(parts):
    rep_count, blk_count = parts.shape[:2]
    blks = [("blk", b) for b in bits_of(blk_count)]
    reps = [("rep", b) for b in bits_of(rep_count)]
    orders = [reps + blks, reps[:1] + blks[:1] + reps[1:] + blks[1:]]
    total = rep_count * blk_count - 1
    piece = parts.shape[2:]
    return pl.pallas_call(
        functools.partial(reduce_kernel, orders),
        out_shape=jax.ShapeDtypeStruct(piece, parts.dtype),
        in_specs=[pl.BlockSpec(memory_space=pltpu.VMEM)],
        out_specs=pl.BlockSpec(memory_space=pltpu.VMEM),
        scratch_shapes=[
            pltpu.VMEM(parts.shape, parts.dtype),
            pltpu.VMEM((total,) + piece, parts.dtype),
            pltpu.SemaphoreType.DMA((len(orders), total)),
            pltpu.SemaphoreType.DMA((len(orders), total)),
        ],
        compiler_params=pltpu.CompilerParams(
            collective_id=1, has_side_effects=True, vmem_limit_bytes=48 * 1024 * 1024
        ),
    )(parts)


def contract_kernel(
    chunk, group, per_owner, cols, trip_ref, count_ref, tab_ref, x_ref, out_ref, fi, fj, fk, y1, y2, y3
):
    s = pl.program_id(0)
    step = pl.program_id(1)
    depth, lanes = tab_ref.shape[2:]
    edge, rank = fi.shape
    fold = lanes // cols
    groups = edge // depth
    lane_group = lax.broadcasted_iota(jnp.int32, (depth, lanes), 1) // cols

    def load_block(index, dest):
        owner = index // per_owner
        for u in range(groups):
            g = (index % per_owner) * groups + u
            for h in range(rank // lanes):
                tile = jnp.zeros((depth, lanes), jnp.float32)
                for m in range(fold):
                    piece = tab_ref[h * fold + m, owner].astype(jnp.float32)
                    moved = pltpu.roll(piece, ((m + fold - g) % fold) * cols, 1)
                    tile = jnp.where(lane_group == m, moved, tile)
                dest[u * depth : (u + 1) * depth, h * lanes : (h + 1) * lanes] = tile.astype(dest.dtype)

    def add_block(index, weight, value):
        owner = index // per_owner
        for u in range(groups):
            g = (index % per_owner) * groups + u
            for h in range(rank // lanes):
                tile = weight * value[u * depth : (u + 1) * depth, h * lanes : (h + 1) * lanes]
                for m in range(fold):
                    moved = pltpu.roll(tile, ((g + fold - m) % fold) * cols, 1)
                    out_ref[h * fold + m, owner] += jnp.where(lane_group == g, moved, 0.0)

    i = trip_ref[s, 0]
    j = trip_ref[s, 1]
    k = trip_ref[s, 2]

    @pl.when(jnp.logical_and(s == 0, step == 0))
    def _():
        out_ref[...] = jnp.zeros_like(out_ref)

    @pl.when(step == 0)
    def _():
        load_block(i, fi)
        load_block(j, fj)
        load_block(k, fk)
        y2[...] = jnp.zeros_like(y2)
        y3[...] = jnp.zeros_like(y3)

    middle = fj[...].astype(jnp.bfloat16)
    lower = fk[...].astype(jnp.bfloat16)

    @pl.loop(0, chunk // group)
    def _(g):
        start = pl.multiple_of(step * chunk + g * group, group)
        scale = fi[pl.ds(start, group), :]
        third = y3[...]
        for u in range(group):
            right = lax.dot_general(
                x_ref[0, g * group + u],
                middle,
                (((0,), (0,)), ((), ())),
                preferred_element_type=jnp.float32,
            )
            third = third + right * scale[u : u + 1, :]
        y3[...] = third
        rows = []
        second = y2[...]
        for u in range(group):
            left = jnp.dot(x_ref[0, g * group + u], lower, preferred_element_type=jnp.float32)
            second = second + left * scale[u : u + 1, :]
            rows.append(jnp.sum(left * fj[...], axis=0, keepdims=True))
        y2[...] = second
        y1[pl.ds(start, group), :] = jnp.concatenate(rows, axis=0)

    @pl.when(step == pl.num_programs(1) - 1)
    def _():
        apart = jnp.logical_and(i != j, j != k)
        every = jnp.logical_and(i == j, j == k)
        base = jnp.where(s < count_ref[0], jnp.where(apart, 2.0, 1.0), 0.0)
        dropped = jnp.where(every, 0.0, base)
        add_block(i, base, y1)
        add_block(j, dropped, y2)
        add_block(k, dropped, y3)


def contract_all(triples, slot_count, table, tensor_blocks, per_owner, cols, rank):
    slots, edge = tensor_blocks.shape[:2]
    chunk = 32
    group = 8
    wide = pltpu.VMEM((edge, rank), jnp.float32)
    return pl.pallas_call(
        functools.partial(contract_kernel, chunk, group, per_owner, cols),
        grid=(slots, edge // chunk),
        out_shape=jax.ShapeDtypeStruct(table.shape, jnp.float32),
        in_specs=[
            pl.BlockSpec(memory_space=pltpu.SMEM),
            pl.BlockSpec(memory_space=pltpu.SMEM),
            pl.BlockSpec(memory_space=pltpu.VMEM),
            pl.BlockSpec((1, chunk, edge, edge), lambda s, t: (s, t, 0, 0)),
        ],
        out_specs=pl.BlockSpec(memory_space=pltpu.VMEM),
        scratch_shapes=[wide] * 6,
        compiler_params=pltpu.CompilerParams(vmem_limit_bytes=48 * 1024 * 1024),
    )(triples, slot_count, table, tensor_blocks)


def shards(tensor_blocks, triples, slot_count, factor):
    rows, cols = factor.shape
    edge = tensor_blocks.shape[1]
    rep_count = lax.axis_size("rep")
    blk_count = lax.axis_size("blk")
    rank = cols * rep_count
    fold = 128 // cols
    depth = rows // fold
    packed = factor.reshape(fold, depth, cols).transpose(1, 0, 2).reshape(depth, fold * cols)
    table = gather_all(packed, rep_count, blk_count)
    parts = contract_all(triples, slot_count, table, tensor_blocks, rows // edge, cols, rank)
    moment = reduce_all(parts)
    moment = moment.reshape(depth, fold, cols).transpose(1, 0, 2).reshape(rows, cols)

    flat = table.reshape(rep_count, blk_count * depth, fold * cols)
    mine = lax.dynamic_index_in_dim(flat, lax.axis_index("rep"), 0, keepdims=False)
    pairs = lax.dot_general(
        flat, mine, (((1,), (0,)), ((), ())), preferred_element_type=jnp.float32
    )
    gram_cols = sum(
        pairs[:, g * cols : (g + 1) * cols, g * cols : (g + 1) * cols] for g in range(fold)
    ).reshape(rank, cols)
    own = lax.dynamic_index_in_dim(table, lax.axis_index("blk"), 1, keepdims=False)
    own_rows = own.reshape(rep_count, depth, fold, cols).transpose(2, 1, 0, 3).reshape(rows, rank)
    fitted = jnp.dot(
        own_rows.astype(jnp.float32),
        gram_cols * gram_cols,
        preferred_element_type=jnp.float32,
        precision=lax.Precision.HIGHEST,
    )
    return fitted - moment


def solution(mesh):
    in_specs = (
        P(("blk", "rep"), None, None, None),
        P(("blk", "rep"), None),
        P(("blk", "rep")),
        P("blk", "rep"),
    )
    out_specs = P("blk", "rep")
    return jax.shard_map(shards, mesh=mesh, in_specs=in_specs, out_specs=out_specs, check_vma=False)
```
